32 devices in a mesh: groups: 2 (over x), section: 4 (over z), seq: 4 (over y, core).
Axes of the slice: x: 2, y: 2, z: 4, core: 2. Of those that a mesh axis runs over, the one named last changes fastest.
Arguments:
- queries: bfloat16 [2048, 4096], P(('groups', 'section', 'seq')), parts along dimension 0, may hold values from -6 to 6
- keys: bfloat16 [2048, 4096], P(('groups', 'section', 'seq')), parts along dimension 0, may hold values from -6 to 6
- values: bfloat16 [2048, 4096], P(('groups', 'section', 'seq')), parts along dimension 0, may hold values from -6 to 6
- query_gain: float32 [4096], replicated, may hold values from 0.1 to 1.9
- key_gain: float32 [4096], replicated, may hold values from 0.1 to 1.9
- placement: int32 [8], P('groups'), parts along dimension 0, may hold values from 0 to 3, each once
- span_mask: int32 [8, 4], P('groups'), parts along dimension 0, may hold values from 0 to 1, as said below
Outputs:
- attended: bfloat16 [2048, 4096], P(('groups', 'section', 'seq')), parts along dimension 0
The draws below stay inside these ranges and needn't reach their ends.
There are 2 independent parts, one for each index of `groups`. The reference program is written for one: setup_inputs(seed, part) draws one part's arguments, and reference() takes and returns one part's arrays. A program takes and returns all parts, laid end to end along the dimension named above; an argument that names none is the same for every part. Nothing has to cross between parts.
Inputs may be any that keep to these rules, and one draw needn't show every extreme that they name: `span_mask`: row a is 1 at column a and 0 at every column after a; the last row is all ones.
All inputs are finite; a program needn't handle non-finite values.
Results may differ from the reference program's by a relative error of at most 0.0038.
The reference program's roundings to bfloat16 on the way (of `normed_q`, `normed_k` and `weights`) count: a program that leaves them out, or rounds other values in their place, can miss the bound.
Values may be sent and summed in bfloat16 or wider, within the bound.
A program may use at most 64 MiB of HBM per device.

```python
import jax
import jax.numpy as jnp
from jax import lax

HEADS = 32
HEAD_DIM = 128
D = 4096
SPAN = 256
SECTIONS = 4
TOKENS = 1024


def draw_queries(key, part):
    key = jax.random.fold_in(key, 1)
    base = jnp.clip(jax.random.normal(key, (TOKENS, D), jnp.float32), -6.0, 6.0)
    return base.astype(jnp.bfloat16)


def draw_keys(key, part):
    key = jax.random.fold_in(key, 2)
    base = jnp.clip(jax.random.normal(key, (TOKENS, D), jnp.float32), -6.0, 6.0)
    return base.astype(jnp.bfloat16)


def draw_span_mask(key, part):
    key = jax.random.fold_in(key, 3)
    order = jnp.arange(SECTIONS, dtype=jnp.int32)
    later = order[:, None]
    earlier = order[None, :]
    coins = jax.random.randint(key, (SECTIONS, SECTIONS), 0, 2, dtype=jnp.int32)
    below = (earlier < later) & (coins == 1)
    diagonal = earlier == later
    last_row = (later == SECTIONS - 1) & (earlier <= later)
    return (below | diagonal | last_row).astype(jnp.int32)


def block_scale(stream_key, dims, cuts, smallest, largest):
    level, own = 1.0, jax.random.fold_in(stream_key, 6)
    for position, blocks in cuts:
        draws = jnp.exp(jax.random.uniform(jax.random.fold_in(own, position), (blocks,), jnp.float32, smallest / len(cuts), largest / len(cuts)))
        level = level * jnp.repeat(draws, dims[position] // blocks).reshape([-1 if axis == position else 1 for axis in range(len(dims))])
    return level


def normal_values(own_key, extent, scale, reach, pieces=(), held_as=jnp.bfloat16):
    values = jax.random.normal(own_key, extent, jnp.float32) * scale
    if len(pieces) > 0:
        values = block_scale(own_key, extent, pieces, -0.22, 0.18) * values
    return jnp.clip(values, min=-reach, max=reach).astype(held_as)


def setup_inputs(seed: int = 0, part: int = 0) -> dict:
    seeds = jax.random.split(jax.random.key(seed), 8)
    part_keys = jax.random.split(jax.random.fold_in(seeds[7], part), 8)
    return {
        "queries": draw_queries(jax.random.fold_in(jax.random.fold_in(seeds[7], part), 71), part),
        "keys": draw_keys(jax.random.fold_in(jax.random.fold_in(seeds[7], part), 71), part),
        "values": normal_values(part_keys[2], (TOKENS, D), 1.0, 6.0, ((0, 16),)),
        "query_gain": jnp.clip(1.0 + 0.18 * jax.random.normal(seeds[3], (D,), jnp.float32), 0.1, 1.9),
        "key_gain": jnp.clip(1.0 + 0.18 * jax.random.normal(seeds[4], (D,), jnp.float32), 0.1, 1.9),
        "placement": jax.random.permutation(part_keys[5], SECTIONS).astype(jnp.int32),
        "span_mask": draw_span_mask(jax.random.fold_in(jax.random.fold_in(seeds[7], part), 71), part),
    }


def normalize(rows, gain):
    floats = rows.astype(jnp.float32)
    factor = lax.rsqrt(lax.optimization_barrier(jnp.mean(floats * floats, axis=-1, keepdims=True)) + 1e-06)
    return (floats * factor * gain.astype(jnp.float32)).astype(jnp.bfloat16)

def reference(queries, keys, values, query_gain, key_gain, placement, span_mask):
    normed_q = normalize(queries, query_gain)
    normed_k = normalize(keys, key_gain)
    span_of = placement[(jnp.arange(TOKENS) // SPAN).astype(jnp.int32)]
    allowed = span_mask[span_of][:, span_of] == 1
    score_scale = 1.0 / HEAD_DIM ** 0.5
    q_heads = normed_q.reshape(TOKENS, HEADS, HEAD_DIM).transpose(1, 0, 2)
    k_heads = normed_k.reshape(TOKENS, HEADS, HEAD_DIM).transpose(1, 0, 2)
    v_heads = values.reshape(TOKENS, HEADS, HEAD_DIM).transpose(1, 0, 2)

    def one_head(operands):
        q_one, k_one, v_one = operands
        scores = jnp.dot(q_one, k_one.T, preferred_element_type=jnp.float32) * score_scale
        scores = jnp.where(allowed, scores, -1e+30)
        top = lax.optimization_barrier(jnp.max(scores, axis=1, keepdims=True))
        weights = jnp.where(allowed, jnp.exp(scores - top), 0.0).astype(jnp.bfloat16)
        totals = lax.optimization_barrier(jnp.sum(weights.astype(jnp.float32), axis=1, keepdims=True))
        summed = jnp.dot(weights, v_one, preferred_element_type=jnp.float32)
        return (summed / totals).astype(jnp.bfloat16)
    heads_out = lax.map(one_head, (q_heads, k_heads, v_heads))
    return heads_out.transpose(1, 0, 2).reshape(TOKENS, D)
```

```python
import functools
import math

import jax
import jax.numpy as jnp
from jax import lax
from jax.experimental import pallas as pl
from jax.experimental.pallas import tpu as pltpu
from jax.sharding import PartitionSpec as P

HEADS = 32
HEAD_DIM = 128
MESH = pl.DeviceIdType.MESH


def flipped(index, flips, count):
    result = index
    bit = 1
    while bit < count:
        result = result + ((flips // bit) % 2) * bit * (1 - 2 * ((index // bit) % 2))
        bit *= 2
    return result


def kernel(
    sections,
    seq_count,
    q_ref,
    k_ref,
    v_ref,
    query_gain,
    key_gain,
    placement,
    span_mask,
    out_ref,
    norm_q,
    norm_k,
    all_q,
    all_k,
    all_v,
    result,
    in_send,
    in_recv,
    out_send,
    out_recv,
    own_sem,
):
    rows = q_ref.shape[0]
    count = sections * seq_count
    own_heads = HEADS // count
    span_len = rows * seq_count
    section = lax.axis_index("section")
    seq = lax.axis_index("seq")
    me = section * seq_count + seq
    first_row = pl.multiple_of(me * rows, rows)

    def peer(step):
        to_section = flipped(section, step // seq_count, sections)
        to_seq = flipped(seq, step % seq_count, seq_count)
        return to_section, to_seq

    def start_of(device, head):
        return pl.multiple_of((device * own_heads + head) * HEAD_DIM, HEAD_DIM)

    barrier = pltpu.get_barrier_semaphore()

    def greet(step, carry):
        to_section, to_seq = peer(step)
        pl.semaphore_signal(
            barrier, inc=1, device_id={"section": to_section, "seq": to_seq}, device_id_type=MESH
        )
        return carry

    lax.fori_loop(1, count, greet, 0)
    all_v[:, :, HEAD_DIM:] = jnp.ones((own_heads, count * rows, HEAD_DIM), jnp.bfloat16)

    def normalize(source, gain, target):
        def chunk(index, carry):
            part = pl.ds(pl.multiple_of(index * 16, 16), 16)
            floats = source[part, :].astype(jnp.float32)
            factor = lax.rsqrt(jnp.mean(floats * floats, axis=-1, keepdims=True) + 1e-06)
            target[part, :] = (floats * factor * gain[...]).astype(jnp.bfloat16)
            return carry

        lax.fori_loop(0, rows // 16, chunk, 0)

    def incoming(which, source, target, head, step):
        to_section, to_seq = peer(step)
        device = to_section * seq_count + to_seq
        return pltpu.make_async_remote_copy(
            src_ref=source.at[:, pl.ds(start_of(device, head), HEAD_DIM)],
            dst_ref=target.at[head, pl.ds(first_row, rows), pl.ds(0, HEAD_DIM)],
            send_sem=in_send.at[which, head, step],
            recv_sem=in_recv.at[which, head, step],
            device_id={"section": to_section, "seq": to_seq},
            device_id_type=MESH,
        )

    def send(which, source, target, head):
        def one(index, carry):
            incoming(which, source, target, head, count - 1 - index).start()
            return carry

        lax.fori_loop(0, count - 1, one, 0)
        target[head, pl.ds(first_row, rows), pl.ds(0, HEAD_DIM)] = source[
            :, pl.ds(start_of(me, head), HEAD_DIM)
        ]

    triples = ((0, v_ref, all_v), (1, norm_k, all_k), (2, norm_q, all_q))
    normalize(k_ref, key_gain, norm_k)
    pl.semaphore_wait(barrier, count - 1)
    send(*triples[0], 0)
    send(*triples[1], 0)
    normalize(q_ref, query_gain, norm_q)
    send(*triples[2], 0)
    for head in range(1, own_heads):
        for triple in triples:
            send(*triple, head)

    def outgoing(head, step):
        to_section, to_seq = peer(step)
        source_row = pl.multiple_of((to_section * seq_count + to_seq) * rows, rows)
        return pltpu.make_async_remote_copy(
            src_ref=result.at[head, pl.ds(source_row, rows), :],
            dst_ref=out_ref.at[:, pl.ds(start_of(me, head), HEAD_DIM)],
            send_sem=out_send.at[head, step],
            recv_sem=out_recv.at[head, step],
            device_id={"section": to_section, "seq": to_seq},
            device_id_type=MESH,
        )

    def kept(head):
        return pltpu.make_async_copy(
            result.at[head, pl.ds(first_row, rows), :],
            out_ref.at[:, pl.ds(start_of(me, head), HEAD_DIM)],
            own_sem.at[head],
        )

    factor = 1.0 / HEAD_DIM**0.5 * math.log2(math.e)

    def attend(head, flips):
        row_section = flipped(section, flips, sections)
        row = pl.multiple_of(row_section * span_len, span_len)
        query = all_q[head, pl.ds(row, span_len), :]
        row_span = placement[row_section]
        scores, shut = [], []
        top = None
        for key_section in range(sections):
            key = all_k[head, key_section * span_len : (key_section + 1) * span_len, :]
            block = lax.dot_general(
                query, key, (((1,), (1,)), ((), ())), preferred_element_type=jnp.float32
            )
            opened = span_mask[row_span, placement[key_section]]
            closed = (opened - 1).astype(jnp.float32) * 1e30
            block_top = jnp.max(block, axis=1, keepdims=True) + closed
            top = block_top if top is None else jnp.maximum(top, block_top)
            scores.append(block)
            shut.append(closed)
        total = jnp.zeros((span_len, 2 * HEAD_DIM), jnp.float32)
        for key_section in range(sections):
            offset = top * factor - shut[key_section]
            weights = jnp.exp2(scores[key_section] * factor - offset).astype(jnp.bfloat16)
            value = all_v[head, key_section * span_len : (key_section + 1) * span_len, :]
            total = total + jnp.dot(weights, value, preferred_element_type=jnp.float32)
        result[head, pl.ds(row, span_len), :] = (
            total[:, :HEAD_DIM] / total[:, HEAD_DIM:]
        ).astype(jnp.bfloat16)

    for head in range(own_heads):

        def arrived(step, carry):
            for triple in triples:
                incoming(*triple, head, step).wait_recv()
            return carry

        lax.fori_loop(1, count, arrived, 0)

        def tile(index, carry):
            flips = sections - 1 - index
            attend(head, flips)

            def give(other, inner):
                step = flips * seq_count + other

                @pl.when(step > 0)
                def _():
                    outgoing(head, step).start()

                return inner

            lax.fori_loop(0, seq_count, give, 0)
            return carry

        lax.fori_loop(0, sections, tile, 0)
        kept(head).start()

    def drain(step, carry):
        for head in range(own_heads):
            for triple in triples:
                incoming(*triple, head, step).wait_send()
            outgoing(head, step).wait()
        return carry

    lax.fori_loop(1, count, drain, 0)
    for head in range(own_heads):
        kept(head).wait()


def spread(queries, keys, values, query_gain, key_gain, placement, span_mask):
    rows, width = queries.shape
    sections, seq_count = lax.axis_size("section"), lax.axis_size("seq")
    count = sections * seq_count
    own_heads = HEADS // count
    tokens = count * rows
    vmem = pl.BlockSpec(memory_space=pltpu.VMEM)
    smem = pl.BlockSpec(memory_space=pltpu.SMEM)
    return pl.pallas_call(
        functools.partial(kernel, sections, seq_count),
        out_shape=jax.ShapeDtypeStruct((rows, width), jnp.bfloat16),
        in_specs=[vmem, vmem, vmem, vmem, vmem, smem, smem],
        out_specs=pl.BlockSpec(memory_space=pl.ANY),
        scratch_shapes=[
            pltpu.VMEM((rows, width), jnp.bfloat16),
            pltpu.VMEM((rows, width), jnp.bfloat16),
            pltpu.VMEM((own_heads, tokens, HEAD_DIM), jnp.bfloat16),
            pltpu.VMEM((own_heads, tokens, HEAD_DIM), jnp.bfloat16),
            pltpu.VMEM((own_heads, tokens, 2 * HEAD_DIM), jnp.bfloat16),
            pltpu.VMEM((own_heads, tokens, HEAD_DIM), jnp.bfloat16),
            pltpu.SemaphoreType.DMA((3, own_heads, count)),
            pltpu.SemaphoreType.DMA((3, own_heads, count)),
            pltpu.SemaphoreType.DMA((own_heads, count)),
            pltpu.SemaphoreType.DMA((own_heads, count)),
            pltpu.SemaphoreType.DMA((own_heads,)),
        ],
        compiler_params=pltpu.CompilerParams(
            collective_id=0, has_side_effects=True, vmem_limit_bytes=40 * 1024 * 1024
        ),
    )(
        queries,
        keys,
        values,
        query_gain.reshape(1, width),
        key_gain.reshape(1, width),
        placement,
        span_mask,
    )


def normalize(rows, gain):
    floats = rows.astype(jnp.float32)
    factor = lax.rsqrt(jnp.mean(floats * floats, axis=-1, keepdims=True) + 1e-06)
    return (floats * factor * gain).astype(jnp.bfloat16)


def body(queries, keys, values, query_gain, key_gain, placement, span_mask):
    tok_rows = queries.shape[0]
    seq_count = lax.axis_size("seq")
    local_heads = HEADS // seq_count
    sections = placement.shape[0]
    span_len = tok_rows * seq_count
    score_scale = 1.0 / HEAD_DIM**0.5
    normed_q = normalize(queries, query_gain).reshape(tok_rows, HEADS, HEAD_DIM)
    normed_k = normalize(keys, key_gain)
    section_ids = jnp.arange(sections, dtype=jnp.int32)
    my_section = lax.axis_index("section")
    my_span = jnp.sum(jnp.where(section_ids == my_section, placement, 0))
    mask_row = jnp.sum(jnp.where((section_ids == my_span)[:, None], span_mask, 0), axis=0)
    section_open = jnp.sum(
        jnp.where(placement[:, None] == section_ids[None, :], mask_row[None, :], 0), axis=1
    )
    initial = (
        jnp.full((local_heads, span_len), -1e30, jnp.float32),
        jnp.zeros((local_heads, span_len), jnp.float32),
        jnp.zeros((span_len, local_heads, HEAD_DIM), jnp.float32),
    )
    window_k, window_v = (
        lax.all_gather(normed_k, "section", axis=0, tiled=True),
        lax.all_gather(values, "section", axis=0, tiled=True),
    )
    window_k = window_k.reshape(sections, tok_rows, HEADS, HEAD_DIM)
    window_v = window_v.reshape(sections, tok_rows, HEADS, HEAD_DIM)
    query_heads = lax.all_to_all(normed_q, "seq", split_axis=1, concat_axis=0, tiled=True)
    heads_k, heads_v = (
        lax.all_to_all(window_k, "seq", split_axis=2, concat_axis=1, tiled=True),
        lax.all_to_all(window_v, "seq", split_axis=2, concat_axis=1, tiled=True),
    )
    heads_k = heads_k.reshape(sections * span_len, local_heads, HEAD_DIM)
    heads_v = heads_v.reshape(sections * span_len, local_heads, HEAD_DIM)
    piece_rows = heads_k.shape[0]
    block_len = math.gcd(piece_rows, 512)
    block_count = piece_rows // block_len
    key_blocks = heads_k.reshape(block_count, block_len, local_heads, HEAD_DIM)
    value_blocks = heads_v.reshape(block_count, block_len, local_heads, HEAD_DIM)
    block_firsts = jnp.arange(block_count, dtype=jnp.int32) * block_len

    def one_block(state_in, block):
        running_max, totals, weighted = state_in
        key_block, value_block, block_first = block
        key_section = (block_first + jnp.arange(block_len, dtype=jnp.int32)) // span_len
        opened = (
            jnp.sum(
                jnp.where(key_section[:, None] == section_ids[None, :], section_open[None, :], 0),
                axis=1,
            )
            > 0
        )
        scores = (
            jnp.einsum("qhd,khd->hqk", query_heads, key_block, preferred_element_type=jnp.float32)
            * score_scale
        )
        scores = jnp.where(opened[None, None, :], scores, -1e30)
        new_max = jnp.maximum(running_max, jnp.max(scores, axis=2))
        weights = jnp.where(
            opened[None, None, :], jnp.exp(scores - new_max[:, :, None]), 0.0
        ).astype(jnp.bfloat16)
        shrink = jnp.exp(running_max - new_max)
        totals = totals * shrink + jnp.sum(weights.astype(jnp.float32), axis=2)
        weighted = weighted * shrink.T[:, :, None] + jnp.einsum(
            "hqk,khd->qhd", weights, value_block, preferred_element_type=jnp.float32
        )
        return ((new_max, totals, weighted), None)

    state_out, unused = lax.scan(one_block, initial, (key_blocks, value_blocks, block_firsts))
    running_max, totals, weighted = state_out
    head_out = (weighted / totals.T[:, :, None]).astype(jnp.bfloat16)
    token_out = lax.all_to_all(head_out, "seq", split_axis=0, concat_axis=1, tiled=True)
    return token_out.reshape(tok_rows, HEADS * HEAD_DIM)


def solution(mesh):
    devices = mesh.shape["section"] * mesh.shape["seq"]
    even = HEADS % devices == 0 and devices & (devices - 1) == 0
    return jax.shard_map(
        spread if even else body,
        mesh=mesh,
        in_specs=(
            P(("groups", "section", "seq"), None),
            P(("groups", "section", "seq"), None),
            P(("groups", "section", "seq"), None),
            P(),
            P(),
            P("groups"),
            P("groups", None),
        ),
        out_specs=P(("groups", "section", "seq"), None),
        check_vma=False,
    )
```

```python
import functools
import math

import jax
import jax.numpy as jnp
from jax import lax
from jax.experimental import pallas as pl
from jax.experimental.pallas import tpu as pltpu
from jax.sharding import PartitionSpec as P

HEADS = 32
HEAD_DIM = 128
MESH = pl.DeviceIdType.MESH


def flipped(index, flips, count):
    result = index
    bit = 1
    while bit < count:
        result = result + ((flips // bit) % 2) * bit * (1 - 2 * ((index // bit) % 2))
        bit *= 2
    return result


def kernel(
    sections,
    seq_count,
    q_ref,
    k_ref,
    v_ref,
    query_gain,
    key_gain,
    placement,
    span_mask,
    out_ref,
    norm_q,
    norm_k,
    all_q,
    all_k,
    all_v,
    result,
    in_send,
    in_recv,
    out_send,
    out_recv,
    own_sem,
):
    rows = q_ref.shape[0]
    count = sections * seq_count
    own_heads = HEADS // count
    span_len = rows * seq_count
    section = lax.axis_index("section")
    seq = lax.axis_index("seq")
    me = section * seq_count + seq
    first_row = pl.multiple_of(me * rows, rows)

    def peer(step):
        to_section = flipped(section, step // seq_count, sections)
        to_seq = flipped(seq, step % seq_count, seq_count)
        return to_section, to_seq

    def columns_of(device):
        width = own_heads * HEAD_DIM
        return pl.ds(pl.multiple_of(device * width, width), width)

    barrier = pltpu.get_barrier_semaphore()

    def greet(step, carry):
        to_section, to_seq = peer(step)
        pl.semaphore_signal(
            barrier, inc=1, device_id={"section": to_section, "seq": to_seq}, device_id_type=MESH
        )
        return carry

    lax.fori_loop(1, count, greet, 0)

    def normalize(source, gain, target):
        def chunk(index, carry):
            part = pl.ds(pl.multiple_of(index * 16, 16), 16)
            floats = source[part, :].astype(jnp.float32)
            factor = lax.rsqrt(jnp.mean(floats * floats, axis=-1, keepdims=True) + 1e-06)
            target[part, :] = (floats * factor * gain[...]).astype(jnp.bfloat16)
            return carry

        lax.fori_loop(0, rows // 16, chunk, 0)

    def incoming(which, source, target, step):
        to_section, to_seq = peer(step)
        return pltpu.make_async_remote_copy(
            src_ref=source.at[:, columns_of(to_section * seq_count + to_seq)],
            dst_ref=target.at[pl.ds(first_row, rows), :],
            send_sem=in_send.at[which, step],
            recv_sem=in_recv.at[which, step],
            device_id={"section": to_section, "seq": to_seq},
            device_id_type=MESH,
        )

    def send(which, source, target):
        def one(index, carry):
            incoming(which, source, target, count - 1 - index).start()
            return carry

        lax.fori_loop(0, count - 1, one, 0)
        target[pl.ds(first_row, rows), :] = source[:, columns_of(me)]

    triples = ((0, v_ref, all_v), (1, norm_k, all_k), (2, norm_q, all_q))
    normalize(k_ref, key_gain, norm_k)
    pl.semaphore_wait(barrier, count - 1)
    send(*triples[0])
    send(*triples[1])
    normalize(q_ref, query_gain, norm_q)
    send(*triples[2])

    def outgoing(step):
        to_section, to_seq = peer(step)
        source_row = pl.multiple_of((to_section * seq_count + to_seq) * rows, rows)
        return pltpu.make_async_remote_copy(
            src_ref=result.at[pl.ds(source_row, rows), :],
            dst_ref=out_ref.at[:, columns_of(me)],
            send_sem=out_send.at[step],
            recv_sem=out_recv.at[step],
            device_id={"section": to_section, "seq": to_seq},
            device_id_type=MESH,
        )

    kept = pltpu.make_async_copy(
        result.at[pl.ds(first_row, rows), :], out_ref.at[:, columns_of(me)], own_sem
    )

    factor = 1.0 / HEAD_DIM**0.5 * math.log2(math.e)

    def attend(head, flips):
        lanes = slice(head * HEAD_DIM, (head + 1) * HEAD_DIM)
        row_section = flipped(section, flips, sections)
        row = pl.multiple_of(row_section * span_len, span_len)
        query = all_q[pl.ds(row, span_len), lanes]
        row_span = placement[row_section]
        scores, shut = [], []
        top = None
        for key_section in range(sections):
            key = all_k[key_section * span_len : (key_section + 1) * span_len, lanes]
            block = lax.dot_general(
                query, key, (((1,), (1,)), ((), ())), preferred_element_type=jnp.float32
            )
            opened = span_mask[row_span, placement[key_section]]
            closed = (opened - 1).astype(jnp.float32) * 1e30
            block_top = jnp.max(block, axis=1, keepdims=True) + closed
            top = block_top if top is None else jnp.maximum(top, block_top)
            scores.append(block)
            shut.append(closed)
        total = jnp.zeros((span_len, 2 * HEAD_DIM), jnp.float32)
        for key_section in range(sections):
            offset = top * factor - shut[key_section]
            weights = jnp.exp2(scores[key_section] * factor - offset).astype(jnp.bfloat16)
            value = all_v[key_section * span_len : (key_section + 1) * span_len, lanes]
            value = jnp.concatenate([value, jnp.ones_like(value)], axis=1)
            total = total + jnp.dot(weights, value, preferred_element_type=jnp.float32)
        result[pl.ds(row, span_len), lanes] = (
            total[:, :HEAD_DIM] / total[:, HEAD_DIM:]
        ).astype(jnp.bfloat16)

    def arrived(step, carry):
        incoming(*triples[0], step).wait_recv()
        incoming(*triples[1], step).wait_recv()
        return carry

    lax.fori_loop(1, count, arrived, 0)

    def tile(index, carry):
        flips = sections - 1 - index

        def take(other, inner):
            step = flips * seq_count + other

            @pl.when(step > 0)
            def _():
                incoming(*triples[2], step).wait_recv()

            return inner

        lax.fori_loop(0, seq_count, take, 0)
        for head in range(own_heads):
            attend(head, flips)

        def give(other, inner):
            step = flips * seq_count + other

            @pl.when(step > 0)
            def _():
                outgoing(step).start()

            return inner

        lax.fori_loop(0, seq_count, give, 0)
        return carry

    lax.fori_loop(0, sections, tile, 0)
    kept.start()

    def drain(step, carry):
        for triple in triples:
            incoming(*triple, step).wait_send()
        outgoing(step).wait()
        return carry

    lax.fori_loop(1, count, drain, 0)
    kept.wait()


def spread(queries, keys, values, query_gain, key_gain, placement, span_mask):
    rows, width = queries.shape
    sections, seq_count = lax.axis_size("section"), lax.axis_size("seq")
    count = sections * seq_count
    own_heads = HEADS // count
    tokens = count * rows
    vmem = pl.BlockSpec(memory_space=pltpu.VMEM)
    smem = pl.BlockSpec(memory_space=pltpu.SMEM)
    return pl.pallas_call(
        functools.partial(kernel, sections, seq_count),
        out_shape=jax.ShapeDtypeStruct((rows, width), jnp.bfloat16),
        in_specs=[vmem, vmem, vmem, vmem, vmem, smem, smem],
        out_specs=pl.BlockSpec(memory_space=pl.ANY),
        scratch_shapes=[
            pltpu.VMEM((rows, width), jnp.bfloat16),
            pltpu.VMEM((rows, width), jnp.bfloat16),
            pltpu.VMEM((tokens, own_heads * HEAD_DIM), jnp.bfloat16),
            pltpu.VMEM((tokens, own_heads * HEAD_DIM), jnp.bfloat16),
            pltpu.VMEM((tokens, own_heads * HEAD_DIM), jnp.bfloat16),
            pltpu.VMEM((tokens, own_heads * HEAD_DIM), jnp.bfloat16),
            pltpu.SemaphoreType.DMA((3, count)),
            pltpu.SemaphoreType.DMA((3, count)),
            pltpu.SemaphoreType.DMA((count,)),
            pltpu.SemaphoreType.DMA((count,)),
            pltpu.SemaphoreType.DMA,
        ],
        compiler_params=pltpu.CompilerParams(
            collective_id=0, has_side_effects=True, vmem_limit_bytes=40 * 1024 * 1024
        ),
    )(
        queries,
        keys,
        values,
        query_gain.reshape(1, width),
        key_gain.reshape(1, width),
        placement,
        span_mask,
    )


def normalize(rows, gain):
    floats = rows.astype(jnp.float32)
    factor = lax.rsqrt(jnp.mean(floats * floats, axis=-1, keepdims=True) + 1e-06)
    return (floats * factor * gain).astype(jnp.bfloat16)


def body(queries, keys, values, query_gain, key_gain, placement, span_mask):
    tok_rows = queries.shape[0]
    seq_count = lax.axis_size("seq")
    local_heads = HEADS // seq_count
    sections = placement.shape[0]
    span_len = tok_rows * seq_count
    score_scale = 1.0 / HEAD_DIM**0.5
    normed_q = normalize(queries, query_gain).reshape(tok_rows, HEADS, HEAD_DIM)
    normed_k = normalize(keys, key_gain)
    section_ids = jnp.arange(sections, dtype=jnp.int32)
    my_section = lax.axis_index("section")
    my_span = jnp.sum(jnp.where(section_ids == my_section, placement, 0))
    mask_row = jnp.sum(jnp.where((section_ids == my_span)[:, None], span_mask, 0), axis=0)
    section_open = jnp.sum(
        jnp.where(placement[:, None] == section_ids[None, :], mask_row[None, :], 0), axis=1
    )
    initial = (
        jnp.full((local_heads, span_len), -1e30, jnp.float32),
        jnp.zeros((local_heads, span_len), jnp.float32),
        jnp.zeros((span_len, local_heads, HEAD_DIM), jnp.float32),
    )
    window_k, window_v = (
        lax.all_gather(normed_k, "section", axis=0, tiled=True),
        lax.all_gather(values, "section", axis=0, tiled=True),
    )
    window_k = window_k.reshape(sections, tok_rows, HEADS, HEAD_DIM)
    window_v = window_v.reshape(sections, tok_rows, HEADS, HEAD_DIM)
    query_heads = lax.all_to_all(normed_q, "seq", split_axis=1, concat_axis=0, tiled=True)
    heads_k, heads_v = (
        lax.all_to_all(window_k, "seq", split_axis=2, concat_axis=1, tiled=True),
        lax.all_to_all(window_v, "seq", split_axis=2, concat_axis=1, tiled=True),
    )
    heads_k = heads_k.reshape(sections * span_len, local_heads, HEAD_DIM)
    heads_v = heads_v.reshape(sections * span_len, local_heads, HEAD_DIM)
    piece_rows = heads_k.shape[0]
    block_len = math.gcd(piece_rows, 512)
    block_count = piece_rows // block_len
    key_blocks = heads_k.reshape(block_count, block_len, local_heads, HEAD_DIM)
    value_blocks = heads_v.reshape(block_count, block_len, local_heads, HEAD_DIM)
    block_firsts = jnp.arange(block_count, dtype=jnp.int32) * block_len

    def one_block(state_in, block):
        running_max, totals, weighted = state_in
        key_block, value_block, block_first = block
        key_section = (block_first + jnp.arange(block_len, dtype=jnp.int32)) // span_len
        opened = (
            jnp.sum(
                jnp.where(key_section[:, None] == section_ids[None, :], section_open[None, :], 0),
                axis=1,
            )
            > 0
        )
        scores = (
            jnp.einsum("qhd,khd->hqk", query_heads, key_block, preferred_element_type=jnp.float32)
            * score_scale
        )
        scores = jnp.where(opened[None, None, :], scores, -1e30)
        new_max = jnp.maximum(running_max, jnp.max(scores, axis=2))
        weights = jnp.where(
            opened[None, None, :], jnp.exp(scores - new_max[:, :, None]), 0.0
        ).astype(jnp.bfloat16)
        shrink = jnp.exp(running_max - new_max)
        totals = totals * shrink + jnp.sum(weights.astype(jnp.float32), axis=2)
        weighted = weighted * shrink.T[:, :, None] + jnp.einsum(
            "hqk,khd->qhd", weights, value_block, preferred_element_type=jnp.float32
        )
        return ((new_max, totals, weighted), None)

    state_out, unused = lax.scan(one_block, initial, (key_blocks, value_blocks, block_firsts))
    running_max, totals, weighted = state_out
    head_out = (weighted / totals.T[:, :, None]).astype(jnp.bfloat16)
    token_out = lax.all_to_all(head_out, "seq", split_axis=0, concat_axis=1, tiled=True)
    return token_out.reshape(tok_rows, HEADS * HEAD_DIM)


def solution(mesh):
    devices = mesh.shape["section"] * mesh.shape["seq"]
    even = HEADS % devices == 0 and devices & (devices - 1) == 0
    return jax.shard_map(
        spread if even else body,
        mesh=mesh,
        in_specs=(
            P(("groups", "section", "seq"), None),
            P(("groups", "section", "seq"), None),
            P(("groups", "section", "seq"), None),
            P(),
            P(),
            P("groups"),
            P("groups", None),
        ),
        out_specs=P(("groups", "section", "seq"), None),
        check_vma=False,
    )
```

```python
import functools
import math

import jax
import jax.numpy as jnp
from jax import lax
from jax.experimental import pallas as pl
from jax.experimental.pallas import tpu as pltpu
from jax.sharding import PartitionSpec as P

HEADS = 32
HEAD_DIM = 128
MESH = pl.DeviceIdType.MESH


def flipped(index, flips, count):
    result = index
    bit = 1
    while bit < count:
        result = result + ((flips // bit) % 2) * bit * (1 - 2 * ((index // bit) % 2))
        bit *= 2
    return result


def kernel(
    sections,
    seq_count,
    q_hbm,
    k_hbm,
    v_ref,
    query_gain_hbm,
    key_gain_hbm,
    placement_hbm,
    span_mask_hbm,
    out_ref,
    q_ref,
    k_ref,
    query_gain,
    key_gain,
    placement,
    span_mask,
    norm_q,
    norm_k,
    all_q,
    all_k,
    all_v,
    result,
    in_send,
    in_recv,
    out_send,
    out_recv,
    own_sem,
    load_sem,
):
    rows = q_ref.shape[0]
    count = sections * seq_count
    own_heads = HEADS // count
    span_len = rows * seq_count
    section = lax.axis_index("section")
    seq = lax.axis_index("seq")
    me = section * seq_count + seq
    first_row = pl.multiple_of(me * rows, rows)

    def peer(step):
        to_section = flipped(section, step // seq_count, sections)
        to_seq = flipped(seq, step % seq_count, seq_count)
        return to_section, to_seq

    def columns_of(device):
        width = own_heads * HEAD_DIM
        return pl.ds(pl.multiple_of(device * width, width), width)

    loads = [
        pltpu.make_async_copy(source, target, load_sem.at[index])
        for index, (source, target) in enumerate(
            (
                (k_hbm, k_ref),
                (key_gain_hbm, key_gain),
                (q_hbm, q_ref),
                (query_gain_hbm, query_gain),
                (placement_hbm, placement),
                (span_mask_hbm, span_mask),
                (v_ref.at[:, columns_of(me)], all_v.at[pl.ds(first_row, rows), :]),
            )
        )
    ]
    barrier = pltpu.get_barrier_semaphore()

    def greet(step, carry):
        to_section, to_seq = peer(step)
        pl.semaphore_signal(
            barrier, inc=1, device_id={"section": to_section, "seq": to_seq}, device_id_type=MESH
        )
        return carry

    lax.fori_loop(1, count, greet, 0)
    for load in loads:
        load.start()

    def normalize(source, gain, target):
        def chunk(index, carry):
            part = pl.ds(pl.multiple_of(index * 16, 16), 16)
            floats = source[part, :].astype(jnp.float32)
            factor = lax.rsqrt(jnp.mean(floats * floats, axis=-1, keepdims=True) + 1e-06)
            target[part, :] = (floats * factor * gain[...]).astype(jnp.bfloat16)
            return carry

        lax.fori_loop(0, rows // 16, chunk, 0)

    def incoming(which, source, target, step):
        to_section, to_seq = peer(step)
        return pltpu.make_async_remote_copy(
            src_ref=source.at[:, columns_of(to_section * seq_count + to_seq)],
            dst_ref=target.at[pl.ds(first_row, rows), :],
            send_sem=in_send.at[which, step],
            recv_sem=in_recv.at[which, step],
            device_id={"section": to_section, "seq": to_seq},
            device_id_type=MESH,
        )

    def send(which, source, target):
        def one(index, carry):
            incoming(which, source, target, count - 1 - index).start()
            return carry

        lax.fori_loop(0, count - 1, one, 0)

    def keep(source, target):
        target[pl.ds(first_row, rows), :] = source[:, columns_of(me)]

    triples = ((0, v_ref, all_v), (1, norm_k, all_k), (2, norm_q, all_q))
    pl.semaphore_wait(barrier, count - 1)
    send(*triples[0])
    loads[0].wait()
    loads[1].wait()
    normalize(k_ref, key_gain, norm_k)
    send(*triples[1])
    loads[2].wait()
    loads[3].wait()
    normalize(q_ref, query_gain, norm_q)
    send(*triples[2])
    keep(norm_k, all_k)
    keep(norm_q, all_q)
    for load in loads[4:]:
        load.wait()

    def outgoing(step):
        to_section, to_seq = peer(step)
        source_row = pl.multiple_of((to_section * seq_count + to_seq) * rows, rows)
        return pltpu.make_async_remote_copy(
            src_ref=result.at[pl.ds(source_row, rows), :],
            dst_ref=out_ref.at[:, columns_of(me)],
            send_sem=out_send.at[step],
            recv_sem=out_recv.at[step],
            device_id={"section": to_section, "seq": to_seq},
            device_id_type=MESH,
        )

    kept = pltpu.make_async_copy(
        result.at[pl.ds(first_row, rows), :], out_ref.at[:, columns_of(me)], own_sem
    )

    factor = 1.0 / HEAD_DIM**0.5 * math.log2(math.e)

    def attend(head, flips):
        lanes = slice(head * HEAD_DIM, (head + 1) * HEAD_DIM)
        row_section = flipped(section, flips, sections)
        row = pl.multiple_of(row_section * span_len, span_len)
        query = all_q[pl.ds(row, span_len), lanes]
        row_span = placement[row_section]
        scores, shut = [], []
        top = None
        for key_section in range(sections):
            key = all_k[key_section * span_len : (key_section + 1) * span_len, lanes]
            block = lax.dot_general(
                query, key, (((1,), (1,)), ((), ())), preferred_element_type=jnp.float32
            )
            opened = span_mask[row_span, placement[key_section]]
            closed = (opened - 1).astype(jnp.float32) * 1e30
            block_top = jnp.max(block, axis=1, keepdims=True) + closed
            top = block_top if top is None else jnp.maximum(top, block_top)
            scores.append(block)
            shut.append(closed)
        total = jnp.zeros((span_len, 2 * HEAD_DIM), jnp.float32)
        for key_section in range(sections):
            offset = top * factor - shut[key_section]
            weights = jnp.exp2(scores[key_section] * factor - offset).astype(jnp.bfloat16)
            value = all_v[key_section * span_len : (key_section + 1) * span_len, lanes]
            value = jnp.concatenate([value, jnp.ones_like(value)], axis=1)
            total = total + jnp.dot(weights, value, preferred_element_type=jnp.float32)
        result[pl.ds(row, span_len), lanes] = (
            total[:, :HEAD_DIM] / total[:, HEAD_DIM:]
        ).astype(jnp.bfloat16)

    def arrived(step, carry):
        incoming(*triples[0], step).wait_recv()
        incoming(*triples[1], step).wait_recv()
        return carry

    lax.fori_loop(1, count, arrived, 0)

    def tile(index, carry):
        flips = sections - 1 - index

        def take(other, inner):
            step = flips * seq_count + other

            @pl.when(step > 0)
            def _():
                incoming(*triples[2], step).wait_recv()

            return inner

        lax.fori_loop(0, seq_count, take, 0)
        for head in range(own_heads):
            attend(head, flips)

        def give(other, inner):
            step = flips * seq_count + other

            @pl.when(step > 0)
            def _():
                outgoing(step).start()

            return inner

        lax.fori_loop(0, seq_count, give, 0)
        return carry

    lax.fori_loop(0, sections, tile, 0)
    kept.start()

    def drain(step, carry):
        for triple in triples:
            incoming(*triple, step).wait_send()
        outgoing(step).wait()
        return carry

    lax.fori_loop(1, count, drain, 0)
    kept.wait()


def spread(queries, keys, values, query_gain, key_gain, placement, span_mask):
    rows, width = queries.shape
    sections, seq_count = lax.axis_size("section"), lax.axis_size("seq")
    count = sections * seq_count
    own_heads = HEADS // count
    tokens = count * rows
    hbm = pl.BlockSpec(memory_space=pltpu.HBM)
    return pl.pallas_call(
        functools.partial(kernel, sections, seq_count),
        out_shape=jax.ShapeDtypeStruct((rows, width), jnp.bfloat16),
        in_specs=[hbm] * 7,
        out_specs=pl.BlockSpec(memory_space=pl.ANY),
        scratch_shapes=[
            pltpu.VMEM((rows, width), jnp.bfloat16),
            pltpu.VMEM((rows, width), jnp.bfloat16),
            pltpu.VMEM((1, width), jnp.float32),
            pltpu.VMEM((1, width), jnp.float32),
            pltpu.SMEM(placement.shape, jnp.int32),
            pltpu.SMEM(span_mask.shape, jnp.int32),
            pltpu.VMEM((rows, width), jnp.bfloat16),
            pltpu.VMEM((rows, width), jnp.bfloat16),
            pltpu.VMEM((tokens, own_heads * HEAD_DIM), jnp.bfloat16),
            pltpu.VMEM((tokens, own_heads * HEAD_DIM), jnp.bfloat16),
            pltpu.VMEM((tokens, own_heads * HEAD_DIM), jnp.bfloat16),
            pltpu.VMEM((tokens, own_heads * HEAD_DIM), jnp.bfloat16),
            pltpu.SemaphoreType.DMA((3, count)),
            pltpu.SemaphoreType.DMA((3, count)),
            pltpu.SemaphoreType.DMA((count,)),
            pltpu.SemaphoreType.DMA((count,)),
            pltpu.SemaphoreType.DMA,
            pltpu.SemaphoreType.DMA((7,)),
        ],
        compiler_params=pltpu.CompilerParams(
            collective_id=0, has_side_effects=True, vmem_limit_bytes=64 * 1024 * 1024
        ),
    )(
        queries,
        keys,
        values,
        query_gain.reshape(1, width),
        key_gain.reshape(1, width),
        placement,
        span_mask,
    )


def normalize(rows, gain):
    floats = rows.astype(jnp.float32)
    factor = lax.rsqrt(jnp.mean(floats * floats, axis=-1, keepdims=True) + 1e-06)
    return (floats * factor * gain).astype(jnp.bfloat16)


def body(queries, keys, values, query_gain, key_gain, placement, span_mask):
    tok_rows = queries.shape[0]
    seq_count = lax.axis_size("seq")
    local_heads = HEADS // seq_count
    sections = placement.shape[0]
    span_len = tok_rows * seq_count
    score_scale = 1.0 / HEAD_DIM**0.5
    normed_q = normalize(queries, query_gain).reshape(tok_rows, HEADS, HEAD_DIM)
    normed_k = normalize(keys, key_gain)
    section_ids = jnp.arange(sections, dtype=jnp.int32)
    my_section = lax.axis_index("section")
    my_span = jnp.sum(jnp.where(section_ids == my_section, placement, 0))
    mask_row = jnp.sum(jnp.where((section_ids == my_span)[:, None], span_mask, 0), axis=0)
    section_open = jnp.sum(
        jnp.where(placement[:, None] == section_ids[None, :], mask_row[None, :], 0), axis=1
    )
    initial = (
        jnp.full((local_heads, span_len), -1e30, jnp.float32),
        jnp.zeros((local_heads, span_len), jnp.float32),
        jnp.zeros((span_len, local_heads, HEAD_DIM), jnp.float32),
    )
    window_k, window_v = (
        lax.all_gather(normed_k, "section", axis=0, tiled=True),
        lax.all_gather(values, "section", axis=0, tiled=True),
    )
    window_k = window_k.reshape(sections, tok_rows, HEADS, HEAD_DIM)
    window_v = window_v.reshape(sections, tok_rows, HEADS, HEAD_DIM)
    query_heads = lax.all_to_all(normed_q, "seq", split_axis=1, concat_axis=0, tiled=True)
    heads_k, heads_v = (
        lax.all_to_all(window_k, "seq", split_axis=2, concat_axis=1, tiled=True),
        lax.all_to_all(window_v, "seq", split_axis=2, concat_axis=1, tiled=True),
    )
    heads_k = heads_k.reshape(sections * span_len, local_heads, HEAD_DIM)
    heads_v = heads_v.reshape(sections * span_len, local_heads, HEAD_DIM)
    piece_rows = heads_k.shape[0]
    block_len = math.gcd(piece_rows, 512)
    block_count = piece_rows // block_len
    key_blocks = heads_k.reshape(block_count, block_len, local_heads, HEAD_DIM)
    value_blocks = heads_v.reshape(block_count, block_len, local_heads, HEAD_DIM)
    block_firsts = jnp.arange(block_count, dtype=jnp.int32) * block_len

    def one_block(state_in, block):
        running_max, totals, weighted = state_in
        key_block, value_block, block_first = block
        key_section = (block_first + jnp.arange(block_len, dtype=jnp.int32)) // span_len
        opened = (
            jnp.sum(
                jnp.where(key_section[:, None] == section_ids[None, :], section_open[None, :], 0),
                axis=1,
            )
            > 0
        )
        scores = (
            jnp.einsum("qhd,khd->hqk", query_heads, key_block, preferred_element_type=jnp.float32)
            * score_scale
        )
        scores = jnp.where(opened[None, None, :], scores, -1e30)
        new_max = jnp.maximum(running_max, jnp.max(scores, axis=2))
        weights = jnp.where(
            opened[None, None, :], jnp.exp(scores - new_max[:, :, None]), 0.0
        ).astype(jnp.bfloat16)
        shrink = jnp.exp(running_max - new_max)
        totals = totals * shrink + jnp.sum(weights.astype(jnp.float32), axis=2)
        weighted = weighted * shrink.T[:, :, None] + jnp.einsum(
            "hqk,khd->qhd", weights, value_block, preferred_element_type=jnp.float32
        )
        return ((new_max, totals, weighted), None)

    state_out, unused = lax.scan(one_block, initial, (key_blocks, value_blocks, block_firsts))
    running_max, totals, weighted = state_out
    head_out = (weighted / totals.T[:, :, None]).astype(jnp.bfloat16)
    token_out = lax.all_to_all(head_out, "seq", split_axis=0, concat_axis=1, tiled=True)
    return token_out.reshape(tok_rows, HEADS * HEAD_DIM)


def solution(mesh):
    devices = mesh.shape["section"] * mesh.shape["seq"]
    even = HEADS % devices == 0 and devices & (devices - 1) == 0
    return jax.shard_map(
        spread if even else body,
        mesh=mesh,
        in_specs=(
            P(("groups", "section", "seq"), None),
            P(("groups", "section", "seq"), None),
            P(("groups", "section", "seq"), None),
            P(),
            P(),
            P("groups"),
            P("groups", None),
        ),
        out_specs=P(("groups", "section", "seq"), None),
        check_vma=False,
    )
```

```python
import functools
import math

import jax
import jax.numpy as jnp
from jax import lax
from jax.experimental import pallas as pl
from jax.experimental.pallas import tpu as pltpu
from jax.sharding import PartitionSpec as P

HEADS = 32
HEAD_DIM = 128
MESH = pl.DeviceIdType.MESH


def flipped(index, flips, count):
    result = index
    bit = 1
    while bit < count:
        result = result + ((flips // bit) % 2) * bit * (1 - 2 * ((index // bit) % 2))
        bit *= 2
    return result


def kernel(
    sections,
    seq_count,
    q_hbm,
    k_hbm,
    v_ref,
    query_gain_hbm,
    key_gain_hbm,
    placement_hbm,
    span_mask_hbm,
    out_ref,
    q_ref,
    k_ref,
    query_gain,
    key_gain,
    placement,
    span_mask,
    norm_q,
    norm_k,
    all_q,
    all_k,
    all_v,
    result,
    in_send,
    in_recv,
    out_send,
    out_recv,
    own_sem,
    load_sem,
):
    rows = q_ref.shape[0]
    count = sections * seq_count
    own_heads = HEADS // count
    span_len = rows * seq_count
    section = lax.axis_index("section")
    seq = lax.axis_index("seq")
    me = section * seq_count + seq
    first_row = pl.multiple_of(me * rows, rows)

    def peer(step):
        to_section = flipped(section, step // seq_count, sections)
        to_seq = flipped(seq, step % seq_count, seq_count)
        return to_section, to_seq

    def columns_of(device):
        width = own_heads * HEAD_DIM
        return pl.ds(pl.multiple_of(device * width, width), width)

    loads = [
        pltpu.make_async_copy(source, target, load_sem.at[index])
        for index, (source, target) in enumerate(
            (
                (k_hbm, k_ref),
                (key_gain_hbm, key_gain),
                (q_hbm, q_ref),
                (query_gain_hbm, query_gain),
                (placement_hbm, placement),
                (span_mask_hbm, span_mask),
                (v_ref.at[:, columns_of(me)], all_v.at[pl.ds(first_row, rows), :]),
            )
        )
    ]
    barrier = pltpu.get_barrier_semaphore()

    def greet(step, carry):
        to_section, to_seq = peer(step)
        pl.semaphore_signal(
            barrier, inc=1, device_id={"section": to_section, "seq": to_seq}, device_id_type=MESH
        )
        return carry

    lax.fori_loop(1, count, greet, 0)
    for load in loads:
        load.start()

    def normalize(source, gain, target):
        def chunk(index, carry):
            part = pl.ds(pl.multiple_of(index * 16, 16), 16)
            floats = source[part, :].astype(jnp.float32)
            factor = lax.rsqrt(jnp.mean(floats * floats, axis=-1, keepdims=True) + 1e-06)
            target[part, :] = (floats * factor * gain[...]).astype(jnp.bfloat16)
            return carry

        lax.fori_loop(0, rows // 16, chunk, 0)

    def incoming(which, source, target, step):
        to_section, to_seq = peer(step)
        return pltpu.make_async_remote_copy(
            src_ref=source.at[:, columns_of(to_section * seq_count + to_seq)],
            dst_ref=target.at[pl.ds(first_row, rows), :],
            send_sem=in_send.at[which, step],
            recv_sem=in_recv.at[which, step],
            device_id={"section": to_section, "seq": to_seq},
            device_id_type=MESH,
        )

    def send(which, source, target):
        def one(index, carry):
            incoming(which, source, target, count - 1 - index).start()
            return carry

        lax.fori_loop(0, count - 1, one, 0)

    def keep(source, target):
        target[pl.ds(first_row, rows), :] = source[:, columns_of(me)]

    triples = ((0, v_ref, all_v), (1, norm_k, all_k), (2, norm_q, all_q))
    pl.semaphore_wait(barrier, count - 1)
    send(*triples[0])
    loads[0].wait()
    loads[1].wait()
    normalize(k_ref, key_gain, norm_k)
    send(*triples[1])
    loads[2].wait()
    loads[3].wait()
    normalize(q_ref, query_gain, norm_q)
    send(*triples[2])
    keep(norm_k, all_k)
    keep(norm_q, all_q)
    for load in loads[4:]:
        load.wait()

    def outgoing(step):
        to_section, to_seq = peer(step)
        source_row = pl.multiple_of((to_section * seq_count + to_seq) * rows, rows)
        return pltpu.make_async_remote_copy(
            src_ref=result.at[pl.ds(source_row, rows), :],
            dst_ref=out_ref.at[:, columns_of(me)],
            send_sem=out_send.at[step],
            recv_sem=out_recv.at[step],
            device_id={"section": to_section, "seq": to_seq},
            device_id_type=MESH,
        )

    kept = pltpu.make_async_copy(
        result.at[pl.ds(first_row, rows), :], out_ref.at[:, columns_of(me)], own_sem
    )

    factor = 1.0 / HEAD_DIM**0.5 * math.log2(math.e)

    def attend(head, flips):
        lanes = slice(head * HEAD_DIM, (head + 1) * HEAD_DIM)
        row_section = flipped(section, flips, sections)
        row = pl.multiple_of(row_section * span_len, span_len)
        query = all_q[pl.ds(row, span_len), lanes]
        row_span = placement[row_section]
        scores, shut = [], []
        top = None
        for key_section in range(sections):
            key = all_k[key_section * span_len : (key_section + 1) * span_len, lanes]
            block = lax.dot_general(
                query, key, (((1,), (1,)), ((), ())), preferred_element_type=jnp.float32
            )
            opened = span_mask[row_span, placement[key_section]]
            closed = (opened - 1).astype(jnp.float32) * 1e30
            block_top = jnp.max(block, axis=1, keepdims=True) + closed
            top = block_top if top is None else jnp.maximum(top, block_top)
            scores.append(block)
            shut.append(closed)
        total = jnp.zeros((span_len, 2 * HEAD_DIM), jnp.float32)
        for key_section in range(sections):
            offset = top * factor - shut[key_section]
            weights = jnp.exp2(scores[key_section] * factor - offset).astype(jnp.bfloat16)
            value = all_v[key_section * span_len : (key_section + 1) * span_len, lanes]
            value = jnp.concatenate([value, jnp.ones_like(value)], axis=1)
            total = total + jnp.dot(weights, value, preferred_element_type=jnp.float32)
        result[pl.ds(row, span_len), lanes] = (
            total[:, :HEAD_DIM] / total[:, HEAD_DIM:]
        ).astype(jnp.bfloat16)

    def arrived(step, carry):
        incoming(*triples[0], step).wait_recv()
        incoming(*triples[1], step).wait_recv()
        return carry

    lax.fori_loop(1, count, arrived, 0)

    def tile(index, carry):
        flips = sections - 1 - index

        def take(other, inner):
            step = flips * seq_count + other

            @pl.when(step > 0)
            def _():
                incoming(*triples[2], step).wait_recv()

            return inner

        lax.fori_loop(0, seq_count, take, 0)
        for head in range(own_heads):
            attend(head, flips)

        def give(other, inner):
            step = flips * seq_count + other

            @pl.when(step > 0)
            def _():
                outgoing(step).start()

            return inner

        lax.fori_loop(0, seq_count, give, 0)
        return carry

    lax.fori_loop(0, sections, tile, 0)
    kept.start()

    def drain(step, carry):
        for triple in triples:
            incoming(*triple, step).wait_send()
        outgoing(step).wait()
        return carry

    lax.fori_loop(1, count, drain, 0)
    kept.wait()


def spread(queries, keys, values, query_gain, key_gain, placement, span_mask):
    rows, width = queries.shape
    sections, seq_count = lax.axis_size("section"), lax.axis_size("seq")
    count = sections * seq_count
    own_heads = HEADS // count
    tokens = count * rows
    hbm = pl.BlockSpec(memory_space=pltpu.HBM)
    return pl.pallas_call(
        functools.partial(kernel, sections, seq_count),
        out_shape=pltpu.VMEM((rows, width), jnp.bfloat16),
        in_specs=[hbm] * 7,
        out_specs=pl.BlockSpec(memory_space=pl.ANY),
        scratch_shapes=[
            pltpu.VMEM((rows, width), jnp.bfloat16),
            pltpu.VMEM((rows, width), jnp.bfloat16),
            pltpu.VMEM((1, width), jnp.float32),
            pltpu.VMEM((1, width), jnp.float32),
            pltpu.SMEM(placement.shape, jnp.int32),
            pltpu.SMEM(span_mask.shape, jnp.int32),
            pltpu.VMEM((rows, width), jnp.bfloat16),
            pltpu.VMEM((rows, width), jnp.bfloat16),
            pltpu.VMEM((tokens, own_heads * HEAD_DIM), jnp.bfloat16),
            pltpu.VMEM((tokens, own_heads * HEAD_DIM), jnp.bfloat16),
            pltpu.VMEM((tokens, own_heads * HEAD_DIM), jnp.bfloat16),
            pltpu.VMEM((tokens, own_heads * HEAD_DIM), jnp.bfloat16),
            pltpu.SemaphoreType.DMA((3, count)),
            pltpu.SemaphoreType.DMA((3, count)),
            pltpu.SemaphoreType.DMA((count,)),
            pltpu.SemaphoreType.DMA((count,)),
            pltpu.SemaphoreType.DMA,
            pltpu.SemaphoreType.DMA((7,)),
        ],
        compiler_params=pltpu.CompilerParams(
            collective_id=0, has_side_effects=True, vmem_limit_bytes=55 * 1024 * 1024
        ),
    )(
        queries,
        keys,
        values,
        query_gain.reshape(1, width),
        key_gain.reshape(1, width),
        placement,
        span_mask,
    )


def normalize(rows, gain):
    floats = rows.astype(jnp.float32)
    factor = lax.rsqrt(jnp.mean(floats * floats, axis=-1, keepdims=True) + 1e-06)
    return (floats * factor * gain).astype(jnp.bfloat16)


def body(queries, keys, values, query_gain, key_gain, placement, span_mask):
    tok_rows = queries.shape[0]
    seq_count = lax.axis_size("seq")
    local_heads = HEADS // seq_count
    sections = placement.shape[0]
    span_len = tok_rows * seq_count
    score_scale = 1.0 / HEAD_DIM**0.5
    normed_q = normalize(queries, query_gain).reshape(tok_rows, HEADS, HEAD_DIM)
    normed_k = normalize(keys, key_gain)
    section_ids = jnp.arange(sections, dtype=jnp.int32)
    my_section = lax.axis_index("section")
    my_span = jnp.sum(jnp.where(section_ids == my_section, placement, 0))
    mask_row = jnp.sum(jnp.where((section_ids == my_span)[:, None], span_mask, 0), axis=0)
    section_open = jnp.sum(
        jnp.where(placement[:, None] == section_ids[None, :], mask_row[None, :], 0), axis=1
    )
    initial = (
        jnp.full((local_heads, span_len), -1e30, jnp.float32),
        jnp.zeros((local_heads, span_len), jnp.float32),
        jnp.zeros((span_len, local_heads, HEAD_DIM), jnp.float32),
    )
    window_k, window_v = (
        lax.all_gather(normed_k, "section", axis=0, tiled=True),
        lax.all_gather(values, "section", axis=0, tiled=True),
    )
    window_k = window_k.reshape(sections, tok_rows, HEADS, HEAD_DIM)
    window_v = window_v.reshape(sections, tok_rows, HEADS, HEAD_DIM)
    query_heads = lax.all_to_all(normed_q, "seq", split_axis=1, concat_axis=0, tiled=True)
    heads_k, heads_v = (
        lax.all_to_all(window_k, "seq", split_axis=2, concat_axis=1, tiled=True),
        lax.all_to_all(window_v, "seq", split_axis=2, concat_axis=1, tiled=True),
    )
    heads_k = heads_k.reshape(sections * span_len, local_heads, HEAD_DIM)
    heads_v = heads_v.reshape(sections * span_len, local_heads, HEAD_DIM)
    piece_rows = heads_k.shape[0]
    block_len = math.gcd(piece_rows, 512)
    block_count = piece_rows // block_len
    key_blocks = heads_k.reshape(block_count, block_len, local_heads, HEAD_DIM)
    value_blocks = heads_v.reshape(block_count, block_len, local_heads, HEAD_DIM)
    block_firsts = jnp.arange(block_count, dtype=jnp.int32) * block_len

    def one_block(state_in, block):
        running_max, totals, weighted = state_in
        key_block, value_block, block_first = block
        key_section = (block_first + jnp.arange(block_len, dtype=jnp.int32)) // span_len
        opened = (
            jnp.sum(
                jnp.where(key_section[:, None] == section_ids[None, :], section_open[None, :], 0),
                axis=1,
            )
            > 0
        )
        scores = (
            jnp.einsum("qhd,khd->hqk", query_heads, key_block, preferred_element_type=jnp.float32)
            * score_scale
        )
        scores = jnp.where(opened[None, None, :], scores, -1e30)
        new_max = jnp.maximum(running_max, jnp.max(scores, axis=2))
        weights = jnp.where(
            opened[None, None, :], jnp.exp(scores - new_max[:, :, None]), 0.0
        ).astype(jnp.bfloat16)
        shrink = jnp.exp(running_max - new_max)
        totals = totals * shrink + jnp.sum(weights.astype(jnp.float32), axis=2)
        weighted = weighted * shrink.T[:, :, None] + jnp.einsum(
            "hqk,khd->qhd", weights, value_block, preferred_element_type=jnp.float32
        )
        return ((new_max, totals, weighted), None)

    state_out, unused = lax.scan(one_block, initial, (key_blocks, value_blocks, block_firsts))
    running_max, totals, weighted = state_out
    head_out = (weighted / totals.T[:, :, None]).astype(jnp.bfloat16)
    token_out = lax.all_to_all(head_out, "seq", split_axis=0, concat_axis=1, tiled=True)
    return token_out.reshape(tok_rows, HEADS * HEAD_DIM)


def solution(mesh):
    devices = mesh.shape["section"] * mesh.shape["seq"]
    even = HEADS % devices == 0 and devices & (devices - 1) == 0
    return jax.shard_map(
        spread if even else body,
        mesh=mesh,
        in_specs=(
            P(("groups", "section", "seq"), None),
            P(("groups", "section", "seq"), None),
            P(("groups", "section", "seq"), None),
            P(),
            P(),
            P("groups"),
            P("groups", None),
        ),
        out_specs=P(("groups", "section", "seq"), None),
        check_vma=False,
    )
```

```python
import functools
import math

import jax
import jax.numpy as jnp
from jax import lax
from jax.experimental import pallas as pl
from jax.experimental.pallas import tpu as pltpu
from jax.sharding import PartitionSpec as P

HEADS = 32
HEAD_DIM = 128
MESH = pl.DeviceIdType.MESH


def flipped(index, flips, count):
    result = index
    bit = 1
    while bit < count:
        result = result + ((flips // bit) % 2) * bit * (1 - 2 * ((index // bit) % 2))
        bit *= 2
    return result


def kernel(
    sections,
    seq_count,
    q_hbm,
    k_hbm,
    v_ref,
    query_gain_hbm,
    key_gain_hbm,
    placement_hbm,
    span_mask_hbm,
    out_ref,
    q_ref,
    k_ref,
    query_gain,
    key_gain,
    placement,
    span_mask,
    norm_q,
    norm_k,
    all_q,
    all_k,
    all_v,
    result,
    in_send,
    in_recv,
    out_send,
    out_recv,
    own_sem,
    load_sem,
):
    rows = q_ref.shape[0]
    count = sections * seq_count
    own_heads = HEADS // count
    span_len = rows * seq_count
    section = lax.axis_index("section")
    seq = lax.axis_index("seq")
    me = section * seq_count + seq
    first_row = pl.multiple_of(me * rows, rows)

    def peer(step):
        to_section = flipped(section, step // seq_count, sections)
        to_seq = flipped(seq, step % seq_count, seq_count)
        return to_section, to_seq

    def columns_of(device):
        width = own_heads * HEAD_DIM
        return pl.ds(pl.multiple_of(device * width, width), width)

    loads = [
        pltpu.make_async_copy(source, target, load_sem.at[index])
        for index, (source, target) in enumerate(
            (
                (k_hbm, k_ref),
                (key_gain_hbm, key_gain),
                (q_hbm, q_ref),
                (query_gain_hbm, query_gain),
                (placement_hbm, placement),
                (span_mask_hbm, span_mask),
                (v_ref.at[:, columns_of(me)], all_v.at[pl.ds(first_row, rows), :]),
            )
        )
    ]
    barrier = pltpu.get_barrier_semaphore()

    def greet(step, carry):
        to_section, to_seq = peer(step)
        pl.semaphore_signal(
            barrier, inc=1, device_id={"section": to_section, "seq": to_seq}, device_id_type=MESH
        )
        return carry

    lax.fori_loop(1, count, greet, 0)
    for load in loads:
        load.start()

    def normalize(source, gain, target):
        def chunk(index, carry):
            part = pl.ds(pl.multiple_of(index * 16, 16), 16)
            floats = source[part, :].astype(jnp.float32)
            factor = lax.rsqrt(jnp.mean(floats * floats, axis=-1, keepdims=True) + 1e-06)
            target[part, :] = (floats * factor * gain[...]).astype(jnp.bfloat16)
            return carry

        lax.fori_loop(0, rows // 16, chunk, 0)

    def incoming(which, source, target, step):
        to_section, to_seq = peer(step)
        return pltpu.make_async_remote_copy(
            src_ref=source.at[:, columns_of(to_section * seq_count + to_seq)],
            dst_ref=target.at[pl.ds(first_row, rows), :],
            send_sem=in_send.at[which, step],
            recv_sem=in_recv.at[which, step],
            device_id={"section": to_section, "seq": to_seq},
            device_id_type=MESH,
        )

    def send(which, source, target):
        def one(index, carry):
            half = count // 2
            far = 1 - index // half
            step = far * (half + index) + (1 - far) * (count - 1 - index)
            incoming(which, source, target, step).start()
            return carry

        lax.fori_loop(0, count - 1, one, 0)

    def keep(source, target):
        target[pl.ds(first_row, rows), :] = source[:, columns_of(me)]

    triples = ((0, v_ref, all_v), (1, norm_k, all_k), (2, norm_q, all_q))
    pl.semaphore_wait(barrier, count - 1)
    send(*triples[0])
    loads[0].wait()
    loads[1].wait()
    normalize(k_ref, key_gain, norm_k)
    send(*triples[1])
    loads[2].wait()
    loads[3].wait()
    normalize(q_ref, query_gain, norm_q)
    send(*triples[2])
    keep(norm_k, all_k)
    keep(norm_q, all_q)
    for load in loads[4:]:
        load.wait()

    def outgoing(step):
        to_section, to_seq = peer(step)
        source_row = pl.multiple_of((to_section * seq_count + to_seq) * rows, rows)
        return pltpu.make_async_remote_copy(
            src_ref=result.at[pl.ds(source_row, rows), :],
            dst_ref=out_ref.at[:, columns_of(me)],
            send_sem=out_send.at[step],
            recv_sem=out_recv.at[step],
            device_id={"section": to_section, "seq": to_seq},
            device_id_type=MESH,
        )

    kept = pltpu.make_async_copy(
        result.at[pl.ds(first_row, rows), :], out_ref.at[:, columns_of(me)], own_sem
    )

    factor = 1.0 / HEAD_DIM**0.5 * math.log2(math.e)

    def attend(head, flips):
        lanes = slice(head * HEAD_DIM, (head + 1) * HEAD_DIM)
        row_section = flipped(section, flips, sections)
        row = pl.multiple_of(row_section * span_len, span_len)
        query = all_q[pl.ds(row, span_len), lanes]
        row_span = placement[row_section]
        scores, shut = [], []
        top = None
        for key_section in range(sections):
            key = all_k[key_section * span_len : (key_section + 1) * span_len, lanes]
            block = lax.dot_general(
                query, key, (((1,), (1,)), ((), ())), preferred_element_type=jnp.float32
            )
            opened = span_mask[row_span, placement[key_section]]
            closed = (opened - 1).astype(jnp.float32) * 1e30
            block_top = jnp.max(block, axis=1, keepdims=True) + closed
            top = block_top if top is None else jnp.maximum(top, block_top)
            scores.append(block)
            shut.append(closed)
        total = jnp.zeros((span_len, 2 * HEAD_DIM), jnp.float32)
        for key_section in range(sections):
            offset = top * factor - shut[key_section]
            weights = jnp.exp2(scores[key_section] * factor - offset).astype(jnp.bfloat16)
            value = all_v[key_section * span_len : (key_section + 1) * span_len, lanes]
            value = jnp.concatenate([value, jnp.ones_like(value)], axis=1)
            total = total + jnp.dot(weights, value, preferred_element_type=jnp.float32)
        result[pl.ds(row, span_len), lanes] = (
            total[:, :HEAD_DIM] / total[:, HEAD_DIM:]
        ).astype(jnp.bfloat16)

    def arrived(step, carry):
        incoming(*triples[0], step).wait_recv()
        incoming(*triples[1], step).wait_recv()
        return carry

    lax.fori_loop(1, count, arrived, 0)

    def tile(index, carry):
        half = max(sections // 2, 1)
        far = 1 - index // half
        flips = far * (half + index) + (1 - far) * (sections - 1 - index)

        def take(other, inner):
            step = flips * seq_count + other

            @pl.when(step > 0)
            def _():
                incoming(*triples[2], step).wait_recv()

            return inner

        lax.fori_loop(0, seq_count, take, 0)
        for head in range(own_heads):
            attend(head, flips)

        def give(other, inner):
            step = flips * seq_count + other

            @pl.when(step > 0)
            def _():
                outgoing(step).start()

            return inner

        lax.fori_loop(0, seq_count, give, 0)
        return carry

    lax.fori_loop(0, sections, tile, 0)
    kept.start()

    def drain(step, carry):
        for triple in triples:
            incoming(*triple, step).wait_send()
        outgoing(step).wait()
        return carry

    lax.fori_loop(1, count, drain, 0)
    kept.wait()


def spread(queries, keys, values, query_gain, key_gain, placement, span_mask):
    rows, width = queries.shape
    sections, seq_count = lax.axis_size("section"), lax.axis_size("seq")
    count = sections * seq_count
    own_heads = HEADS // count
    tokens = count * rows
    hbm = pl.BlockSpec(memory_space=pltpu.HBM)
    return pl.pallas_call(
        functools.partial(kernel, sections, seq_count),
        out_shape=pltpu.VMEM((rows, width), jnp.bfloat16),
        in_specs=[hbm] * 7,
        out_specs=pl.BlockSpec(memory_space=pl.ANY),
        scratch_shapes=[
            pltpu.VMEM((rows, width), jnp.bfloat16),
            pltpu.VMEM((rows, width), jnp.bfloat16),
            pltpu.VMEM((1, width), jnp.float32),
            pltpu.VMEM((1, width), jnp.float32),
            pltpu.SMEM(placement.shape, jnp.int32),
            pltpu.SMEM(span_mask.shape, jnp.int32),
            pltpu.VMEM((rows, width), jnp.bfloat16),
            pltpu.VMEM((rows, width), jnp.bfloat16),
            pltpu.VMEM((tokens, own_heads * HEAD_DIM), jnp.bfloat16),
            pltpu.VMEM((tokens, own_heads * HEAD_DIM), jnp.bfloat16),
            pltpu.VMEM((tokens, own_heads * HEAD_DIM), jnp.bfloat16),
            pltpu.VMEM((tokens, own_heads * HEAD_DIM), jnp.bfloat16),
            pltpu.SemaphoreType.DMA((3, count)),
            pltpu.SemaphoreType.DMA((3, count)),
            pltpu.SemaphoreType.DMA((count,)),
            pltpu.SemaphoreType.DMA((count,)),
            pltpu.SemaphoreType.DMA,
            pltpu.SemaphoreType.DMA((7,)),
        ],
        compiler_params=pltpu.CompilerParams(
            collective_id=0, has_side_effects=True, vmem_limit_bytes=55 * 1024 * 1024
        ),
    )(
        queries,
        keys,
        values,
        query_gain.reshape(1, width),
        key_gain.reshape(1, width),
        placement,
        span_mask,
    )


def normalize(rows, gain):
    floats = rows.astype(jnp.float32)
    factor = lax.rsqrt(jnp.mean(floats * floats, axis=-1, keepdims=True) + 1e-06)
    return (floats * factor * gain).astype(jnp.bfloat16)


def body(queries, keys, values, query_gain, key_gain, placement, span_mask):
    tok_rows = queries.shape[0]
    seq_count = lax.axis_size("seq")
    local_heads = HEADS // seq_count
    sections = placement.shape[0]
    span_len = tok_rows * seq_count
    score_scale = 1.0 / HEAD_DIM**0.5
    normed_q = normalize(queries, query_gain).reshape(tok_rows, HEADS, HEAD_DIM)
    normed_k = normalize(keys, key_gain)
    section_ids = jnp.arange(sections, dtype=jnp.int32)
    my_section = lax.axis_index("section")
    my_span = jnp.sum(jnp.where(section_ids == my_section, placement, 0))
    mask_row = jnp.sum(jnp.where((section_ids == my_span)[:, None], span_mask, 0), axis=0)
    section_open = jnp.sum(
        jnp.where(placement[:, None] == section_ids[None, :], mask_row[None, :], 0), axis=1
    )
    initial = (
        jnp.full((local_heads, span_len), -1e30, jnp.float32),
        jnp.zeros((local_heads, span_len), jnp.float32),
        jnp.zeros((span_len, local_heads, HEAD_DIM), jnp.float32),
    )
    window_k, window_v = (
        lax.all_gather(normed_k, "section", axis=0, tiled=True),
        lax.all_gather(values, "section", axis=0, tiled=True),
    )
    window_k = window_k.reshape(sections, tok_rows, HEADS, HEAD_DIM)
    window_v = window_v.reshape(sections, tok_rows, HEADS, HEAD_DIM)
    query_heads = lax.all_to_all(normed_q, "seq", split_axis=1, concat_axis=0, tiled=True)
    heads_k, heads_v = (
        lax.all_to_all(window_k, "seq", split_axis=2, concat_axis=1, tiled=True),
        lax.all_to_all(window_v, "seq", split_axis=2, concat_axis=1, tiled=True),
    )
    heads_k = heads_k.reshape(sections * span_len, local_heads, HEAD_DIM)
    heads_v = heads_v.reshape(sections * span_len, local_heads, HEAD_DIM)
    piece_rows = heads_k.shape[0]
    block_len = math.gcd(piece_rows, 512)
    block_count = piece_rows // block_len
    key_blocks = heads_k.reshape(block_count, block_len, local_heads, HEAD_DIM)
    value_blocks = heads_v.reshape(block_count, block_len, local_heads, HEAD_DIM)
    block_firsts = jnp.arange(block_count, dtype=jnp.int32) * block_len

    def one_block(state_in, block):
        running_max, totals, weighted = state_in
        key_block, value_block, block_first = block
        key_section = (block_first + jnp.arange(block_len, dtype=jnp.int32)) // span_len
        opened = (
            jnp.sum(
                jnp.where(key_section[:, None] == section_ids[None, :], section_open[None, :], 0),
                axis=1,
            )
            > 0
        )
        scores = (
            jnp.einsum("qhd,khd->hqk", query_heads, key_block, preferred_element_type=jnp.float32)
            * score_scale
        )
        scores = jnp.where(opened[None, None, :], scores, -1e30)
        new_max = jnp.maximum(running_max, jnp.max(scores, axis=2))
        weights = jnp.where(
            opened[None, None, :], jnp.exp(scores - new_max[:, :, None]), 0.0
        ).astype(jnp.bfloat16)
        shrink = jnp.exp(running_max - new_max)
        totals = totals * shrink + jnp.sum(weights.astype(jnp.float32), axis=2)
        weighted = weighted * shrink.T[:, :, None] + jnp.einsum(
            "hqk,khd->qhd", weights, value_block, preferred_element_type=jnp.float32
        )
        return ((new_max, totals, weighted), None)

    state_out, unused = lax.scan(one_block, initial, (key_blocks, value_blocks, block_firsts))
    running_max, totals, weighted = state_out
    head_out = (weighted / totals.T[:, :, None]).astype(jnp.bfloat16)
    token_out = lax.all_to_all(head_out, "seq", split_axis=0, concat_axis=1, tiled=True)
    return token_out.reshape(tok_rows, HEADS * HEAD_DIM)


def solution(mesh):
    devices = mesh.shape["section"] * mesh.shape["seq"]
    even = HEADS % devices == 0 and devices & (devices - 1) == 0
    return jax.shard_map(
        spread if even else body,
        mesh=mesh,
        in_specs=(
            P(("groups", "section", "seq"), None),
            P(("groups", "section", "seq"), None),
            P(("groups", "section", "seq"), None),
            P(),
            P(),
            P("groups"),
            P("groups", None),
        ),
        out_specs=P(("groups", "section", "seq"), None),
        check_vma=False,
    )
```

```python
import functools
import math

import jax
import jax.numpy as jnp
from jax import lax
from jax.experimental import pallas as pl
from jax.experimental.pallas import tpu as pltpu
from jax.sharding import PartitionSpec as P

HEADS = 32
HEAD_DIM = 128
MESH = pl.DeviceIdType.MESH


def flipped(index, flips, count):
    result = index
    bit = 1
    while bit < count:
        result = result + ((flips // bit) % 2) * bit * (1 - 2 * ((index // bit) % 2))
        bit *= 2
    return result


def kernel(
    sections,
    seq_count,
    q_hbm,
    k_hbm,
    v_ref,
    query_gain_hbm,
    key_gain_hbm,
    placement_hbm,
    span_mask_hbm,
    out_ref,
    q_ref,
    k_ref,
    query_gain,
    key_gain,
    placement,
    span_mask,
    norm_q,
    norm_k,
    all_q,
    all_k,
    all_v,
    result,
    in_send,
    in_recv,
    out_send,
    out_recv,
    own_sem,
    load_sem,
):
    rows = q_ref.shape[0]
    count = sections * seq_count
    own_heads = HEADS // count
    span_len = rows * seq_count
    section = lax.axis_index("section")
    seq = lax.axis_index("seq")
    me = section * seq_count + seq
    first_row = pl.multiple_of(me * rows, rows)

    def peer(step):
        to_section = flipped(section, step // seq_count, sections)
        to_seq = flipped(seq, step % seq_count, seq_count)
        return to_section, to_seq

    def columns_of(device):
        width = own_heads * HEAD_DIM
        return pl.ds(pl.multiple_of(device * width, width), width)

    loads = [
        pltpu.make_async_copy(source, target, load_sem.at[index])
        for index, (source, target) in enumerate(
            (
                (k_hbm, k_ref),
                (key_gain_hbm, key_gain),
                (q_hbm, q_ref),
                (query_gain_hbm, query_gain),
                (placement_hbm, placement),
                (span_mask_hbm, span_mask),
                (v_ref.at[:, columns_of(me)], all_v.at[pl.ds(first_row, rows), :]),
            )
        )
    ]
    barrier = pltpu.get_barrier_semaphore()

    def greet(step, carry):
        to_section, to_seq = peer(step)
        pl.semaphore_signal(
            barrier, inc=1, device_id={"section": to_section, "seq": to_seq}, device_id_type=MESH
        )
        return carry

    for step in range(count - 1, 0, -1):
        greet(step, 0)
    for load in loads:
        load.start()

    def normalize(source, gain, target):
        def chunk(index, carry):
            part = pl.ds(pl.multiple_of(index * 16, 16), 16)
            floats = source[part, :].astype(jnp.float32)
            factor = lax.rsqrt(jnp.mean(floats * floats, axis=-1, keepdims=True) + 1e-06)
            target[part, :] = (floats * factor * gain[...]).astype(jnp.bfloat16)
            return carry

        lax.fori_loop(0, rows // 16, chunk, 0)

    def incoming(which, source, target, step):
        to_section, to_seq = peer(step)
        return pltpu.make_async_remote_copy(
            src_ref=source.at[:, columns_of(to_section * seq_count + to_seq)],
            dst_ref=target.at[pl.ds(first_row, rows), :],
            send_sem=in_send.at[which, step],
            recv_sem=in_recv.at[which, step],
            device_id={"section": to_section, "seq": to_seq},
            device_id_type=MESH,
        )

    def send(which, source, target):
        def one(index, carry):
            half = count // 2
            far = 1 - index // half
            step = far * (half + index) + (1 - far) * (count - 1 - index)
            incoming(which, source, target, step).start()
            return carry

        lax.fori_loop(0, count - 1, one, 0)

    def keep(source, target):
        target[pl.ds(first_row, rows), :] = source[:, columns_of(me)]

    triples = ((0, v_ref, all_v), (1, norm_k, all_k), (2, norm_q, all_q))
    pl.semaphore_wait(barrier, count - 1)
    send(*triples[0])
    loads[0].wait()
    loads[1].wait()
    normalize(k_ref, key_gain, norm_k)
    send(*triples[1])
    loads[2].wait()
    loads[3].wait()
    normalize(q_ref, query_gain, norm_q)
    send(*triples[2])
    keep(norm_k, all_k)
    keep(norm_q, all_q)
    for load in loads[4:]:
        load.wait()

    def outgoing(step):
        to_section, to_seq = peer(step)
        source_row = pl.multiple_of((to_section * seq_count + to_seq) * rows, rows)
        return pltpu.make_async_remote_copy(
            src_ref=result.at[pl.ds(source_row, rows), :],
            dst_ref=out_ref.at[:, columns_of(me)],
            send_sem=out_send.at[step],
            recv_sem=out_recv.at[step],
            device_id={"section": to_section, "seq": to_seq},
            device_id_type=MESH,
        )

    kept = pltpu.make_async_copy(
        result.at[pl.ds(first_row, rows), :], out_ref.at[:, columns_of(me)], own_sem
    )

    factor = 1.0 / HEAD_DIM**0.5 * math.log2(math.e)

    def attend(head, flips):
        lanes = slice(head * HEAD_DIM, (head + 1) * HEAD_DIM)
        row_section = flipped(section, flips, sections)
        row = pl.multiple_of(row_section * span_len, span_len)
        query = all_q[pl.ds(row, span_len), lanes]
        row_span = placement[row_section]
        scores, shut = [], []
        top = None
        for key_section in range(sections):
            key = all_k[key_section * span_len : (key_section + 1) * span_len, lanes]
            block = lax.dot_general(
                query, key, (((1,), (1,)), ((), ())), preferred_element_type=jnp.float32
            )
            opened = span_mask[row_span, placement[key_section]]
            closed = (opened - 1).astype(jnp.float32) * 1e30
            block_top = jnp.max(block, axis=1, keepdims=True) + closed
            top = block_top if top is None else jnp.maximum(top, block_top)
            scores.append(block)
            shut.append(closed)
        total = jnp.zeros((span_len, 2 * HEAD_DIM), jnp.float32)
        for key_section in range(sections):
            offset = top * factor - shut[key_section]
            weights = jnp.exp2(scores[key_section] * factor - offset).astype(jnp.bfloat16)
            value = all_v[key_section * span_len : (key_section + 1) * span_len, lanes]
            value = jnp.concatenate([value, jnp.ones_like(value)], axis=1)
            total = total + jnp.dot(weights, value, preferred_element_type=jnp.float32)
        result[pl.ds(row, span_len), lanes] = (
            total[:, :HEAD_DIM] / total[:, HEAD_DIM:]
        ).astype(jnp.bfloat16)

    def arrived(step, carry):
        incoming(*triples[0], step).wait_recv()
        incoming(*triples[1], step).wait_recv()
        return carry

    lax.fori_loop(1, count, arrived, 0)

    def tile(index, carry):
        half = max(sections // 2, 1)
        far = 1 - index // half
        flips = far * (half + index) + (1 - far) * (sections - 1 - index)

        def take(other, inner):
            step = flips * seq_count + other

            @pl.when(step > 0)
            def _():
                incoming(*triples[2], step).wait_recv()

            return inner

        lax.fori_loop(0, seq_count, take, 0)
        for head in range(own_heads):
            attend(head, flips)

        def give(other, inner):
            step = flips * seq_count + other

            @pl.when(step > 0)
            def _():
                outgoing(step).start()

            return inner

        lax.fori_loop(0, seq_count, give, 0)
        return carry

    lax.fori_loop(0, sections, tile, 0)
    kept.start()

    def drain(step, carry):
        for triple in triples:
            incoming(*triple, step).wait_send()
        outgoing(step).wait()
        return carry

    lax.fori_loop(1, count, drain, 0)
    kept.wait()


def spread(queries, keys, values, query_gain, key_gain, placement, span_mask):
    rows, width = queries.shape
    sections, seq_count = lax.axis_size("section"), lax.axis_size("seq")
    count = sections * seq_count
    own_heads = HEADS // count
    tokens = count * rows
    hbm = pl.BlockSpec(memory_space=pltpu.HBM)
    return pl.pallas_call(
        functools.partial(kernel, sections, seq_count),
        out_shape=pltpu.VMEM((rows, width), jnp.bfloat16),
        in_specs=[hbm] * 7,
        out_specs=pl.BlockSpec(memory_space=pl.ANY),
        scratch_shapes=[
            pltpu.VMEM((rows, width), jnp.bfloat16),
            pltpu.VMEM((rows, width), jnp.bfloat16),
            pltpu.VMEM((1, width), jnp.float32),
            pltpu.VMEM((1, width), jnp.float32),
            pltpu.SMEM(placement.shape, jnp.int32),
            pltpu.SMEM(span_mask.shape, jnp.int32),
            pltpu.VMEM((rows, width), jnp.bfloat16),
            pltpu.VMEM((rows, width), jnp.bfloat16),
            pltpu.VMEM((tokens, own_heads * HEAD_DIM), jnp.bfloat16),
            pltpu.VMEM((tokens, own_heads * HEAD_DIM), jnp.bfloat16),
            pltpu.VMEM((tokens, own_heads * HEAD_DIM), jnp.bfloat16),
            pltpu.VMEM((tokens, own_heads * HEAD_DIM), jnp.bfloat16),
            pltpu.SemaphoreType.DMA((3, count)),
            pltpu.SemaphoreType.DMA((3, count)),
            pltpu.SemaphoreType.DMA((count,)),
            pltpu.SemaphoreType.DMA((count,)),
            pltpu.SemaphoreType.DMA,
            pltpu.SemaphoreType.DMA((7,)),
        ],
        compiler_params=pltpu.CompilerParams(
            collective_id=0, has_side_effects=True, vmem_limit_bytes=55 * 1024 * 1024
        ),
    )(
        queries,
        keys,
        values,
        query_gain.reshape(1, width),
        key_gain.reshape(1, width),
        placement,
        span_mask,
    )


def normalize(rows, gain):
    floats = rows.astype(jnp.float32)
    factor = lax.rsqrt(jnp.mean(floats * floats, axis=-1, keepdims=True) + 1e-06)
    return (floats * factor * gain).astype(jnp.bfloat16)


def body(queries, keys, values, query_gain, key_gain, placement, span_mask):
    tok_rows = queries.shape[0]
    seq_count = lax.axis_size("seq")
    local_heads = HEADS // seq_count
    sections = placement.shape[0]
    span_len = tok_rows * seq_count
    score_scale = 1.0 / HEAD_DIM**0.5
    normed_q = normalize(queries, query_gain).reshape(tok_rows, HEADS, HEAD_DIM)
    normed_k = normalize(keys, key_gain)
    section_ids = jnp.arange(sections, dtype=jnp.int32)
    my_section = lax.axis_index("section")
    my_span = jnp.sum(jnp.where(section_ids == my_section, placement, 0))
    mask_row = jnp.sum(jnp.where((section_ids == my_span)[:, None], span_mask, 0), axis=0)
    section_open = jnp.sum(
        jnp.where(placement[:, None] == section_ids[None, :], mask_row[None, :], 0), axis=1
    )
    initial = (
        jnp.full((local_heads, span_len), -1e30, jnp.float32),
        jnp.zeros((local_heads, span_len), jnp.float32),
        jnp.zeros((span_len, local_heads, HEAD_DIM), jnp.float32),
    )
    window_k, window_v = (
        lax.all_gather(normed_k, "section", axis=0, tiled=True),
        lax.all_gather(values, "section", axis=0, tiled=True),
    )
    window_k = window_k.reshape(sections, tok_rows, HEADS, HEAD_DIM)
    window_v = window_v.reshape(sections, tok_rows, HEADS, HEAD_DIM)
    query_heads = lax.all_to_all(normed_q, "seq", split_axis=1, concat_axis=0, tiled=True)
    heads_k, heads_v = (
        lax.all_to_all(window_k, "seq", split_axis=2, concat_axis=1, tiled=True),
        lax.all_to_all(window_v, "seq", split_axis=2, concat_axis=1, tiled=True),
    )
    heads_k = heads_k.reshape(sections * span_len, local_heads, HEAD_DIM)
    heads_v = heads_v.reshape(sections * span_len, local_heads, HEAD_DIM)
    piece_rows = heads_k.shape[0]
    block_len = math.gcd(piece_rows, 512)
    block_count = piece_rows // block_len
    key_blocks = heads_k.reshape(block_count, block_len, local_heads, HEAD_DIM)
    value_blocks = heads_v.reshape(block_count, block_len, local_heads, HEAD_DIM)
    block_firsts = jnp.arange(block_count, dtype=jnp.int32) * block_len

    def one_block(state_in, block):
        running_max, totals, weighted = state_in
        key_block, value_block, block_first = block
        key_section = (block_first + jnp.arange(block_len, dtype=jnp.int32)) // span_len
        opened = (
            jnp.sum(
                jnp.where(key_section[:, None] == section_ids[None, :], section_open[None, :], 0),
                axis=1,
            )
            > 0
        )
        scores = (
            jnp.einsum("qhd,khd->hqk", query_heads, key_block, preferred_element_type=jnp.float32)
            * score_scale
        )
        scores = jnp.where(opened[None, None, :], scores, -1e30)
        new_max = jnp.maximum(running_max, jnp.max(scores, axis=2))
        weights = jnp.where(
            opened[None, None, :], jnp.exp(scores - new_max[:, :, None]), 0.0
        ).astype(jnp.bfloat16)
        shrink = jnp.exp(running_max - new_max)
        totals = totals * shrink + jnp.sum(weights.astype(jnp.float32), axis=2)
        weighted = weighted * shrink.T[:, :, None] + jnp.einsum(
            "hqk,khd->qhd", weights, value_block, preferred_element_type=jnp.float32
        )
        return ((new_max, totals, weighted), None)

    state_out, unused = lax.scan(one_block, initial, (key_blocks, value_blocks, block_firsts))
    running_max, totals, weighted = state_out
    head_out = (weighted / totals.T[:, :, None]).astype(jnp.bfloat16)
    token_out = lax.all_to_all(head_out, "seq", split_axis=0, concat_axis=1, tiled=True)
    return token_out.reshape(tok_rows, HEADS * HEAD_DIM)


def solution(mesh):
    devices = mesh.shape["section"] * mesh.shape["seq"]
    even = HEADS % devices == 0 and devices & (devices - 1) == 0
    return jax.shard_map(
        spread if even else body,
        mesh=mesh,
        in_specs=(
            P(("groups", "section", "seq"), None),
            P(("groups", "section", "seq"), None),
            P(("groups", "section", "seq"), None),
            P(),
            P(),
            P("groups"),
            P("groups", None),
        ),
        out_specs=P(("groups", "section", "seq"), None),
        check_vma=False,
    )
```
